32 devices in a mesh: branch: 4 (over y, x), seq: 8 (over z, core).
Axes of the slice: x: 2, y: 2, z: 4, core: 2. Of those that a mesh axis runs over, the one named last changes fastest.
Arguments:
- query: bfloat16 [4, 1024, 8192], P('branch', 'seq'), may hold values from -150 to 150
- key_new: bfloat16 [4, 1024, 1024], P('branch', 'seq'), may hold values from -6 to 6
- value_new: bfloat16 [4, 1024, 1024], P('branch', 'seq'), may hold values from -18 to 18
- hist_key: bfloat16 [128, 1024], P('seq'), may hold values from -6 to 6
- hist_value: bfloat16 [128, 1024], P('seq'), may hold values from -18 to 18
- sib_source: int32 [4, 4], replicated, may hold values from 0 to 3, as said below
- sib_block: int32 [4, 4], replicated, may hold values from 0 to 3, as said below
- sib_mask: int32 [4, 4, 4], replicated, may hold values 0 or 1
Outputs:
- attended: bfloat16 [4, 1024, 8192], P('branch', 'seq')
The draws below stay inside these ranges and needn't reach their ends.
Inputs may be any that keep to these rules, and one draw needn't show every extreme that they name: `sib_source`: never the reader itself. In every reader's list exactly 2 slots name one source and no source is named more than 2 times. `sib_block`: A reader lists no block of one source twice.
All inputs are finite; a program needn't handle non-finite values.
Results may differ from the reference program's by a relative error of at most 0.0036.
Values may be sent and summed in bfloat16 or wider, within the bound.
A program may use at most 128 MiB of HBM per device.

```python
import math
import jax
import jax.numpy as jnp
from jax import lax

QH = 64
KVH = 8
HD = 128
BLOCK = 256
NSIB = 4
SRCMAX = 2
BRANCHES = 4
OWN_LEN = 1024
HIST = 128
NBLK = 4


def history_base(key):
    raw = jax.random.normal(jax.random.fold_in(key, 7), (HIST, KVH * HD), jnp.float32)
    raw = jnp.clip(raw, -6.0, 6.0)
    return raw


def draw_hist_key(key, part):
    return history_base(key).astype(jnp.bfloat16)


def draw_query(key, part):
    base = jax.random.normal(jax.random.fold_in(key, 13), (BRANCHES, OWN_LEN, QH * HD), jnp.float32)
    base = jnp.clip(2.0 * base, -12.0, 12.0)
    return base.astype(jnp.bfloat16)


def sibling_lists(key):
    base = jax.random.fold_in(key, 31)
    heavy = jax.random.randint(jax.random.fold_in(base, 1), (BRANCHES,), 1, 4)
    second = jnp.where(heavy == 1, 2, 1)
    third = jnp.where(heavy == 3, 2, 3)
    split = jax.random.randint(jax.random.fold_in(base, 2), (BRANCHES,), 0, SRCMAX)
    slots = jnp.arange(NSIB, dtype=jnp.int32)[None, :]
    offset = jnp.where(slots < SRCMAX, heavy[:, None], jnp.where(slots < SRCMAX + split[:, None], second[:, None], third[:, None]))
    within = jnp.where(slots < SRCMAX, slots, jnp.where(slots < SRCMAX + split[:, None], slots - SRCMAX, slots - SRCMAX - split[:, None]))

    def one_order(order_key):
        return jax.random.permutation(order_key, NBLK)
    orders = jax.vmap(one_order)(jax.random.split(jax.random.fold_in(base, 3), BRANCHES * 3)).reshape(BRANCHES, 3, NBLK)
    readers = jnp.arange(BRANCHES, dtype=jnp.int32)[:, None]
    blocks = orders[readers, offset - 1, within]
    sources = (readers + offset) % BRANCHES

    def one_shuffle(order_key):
        return jax.random.permutation(order_key, NSIB)
    shuffle = jax.vmap(one_shuffle)(jax.random.split(jax.random.fold_in(base, 4), BRANCHES))
    sources = jnp.take_along_axis(sources, shuffle, axis=1)
    blocks = jnp.take_along_axis(blocks, shuffle, axis=1)
    return (sources.astype(jnp.int32), blocks.astype(jnp.int32))


def draw_sib_source(key, part):
    return sibling_lists(key)[0]


def draw_sib_block(key, part):
    return sibling_lists(key)[1]


def place_ends(values, rng, smallest, high):
    extent = values.shape
    index_at = [jax.random.randint(jax.random.fold_in(rng, axis), (), 0, extent[axis]) for axis in range(len(extent))]
    values = values.at[tuple(index_at)].set(smallest)
    longest = extent.index(max(extent))
    index_at[longest] = (index_at[longest] + 1) % extent[longest]
    return values.at[tuple(index_at)].set(high)


def block_scale(key, shape, pieces, low, high):
    gain = 1.0
    for axis_at, blocks in pieces:
        draws = jax.random.uniform(jax.random.fold_in(jax.random.fold_in(key, 6), axis_at), (blocks,), jnp.float32, low / len(pieces), high / len(pieces))
        gain = gain * jnp.repeat(jnp.exp(draws), shape[axis_at] // blocks).reshape((-1,) + (1,) * (len(shape) - 1 - axis_at))
    return gain


def normal_values(stream_key, extent, deviation, limit, shards=(), kind=jnp.bfloat16):
    drawn = deviation * jax.random.normal(stream_key, extent, jnp.float32)
    if shards:
        drawn = drawn * block_scale(stream_key, extent, shards, -0.22, 0.18)
    return jnp.clip(drawn, -limit, limit).astype(kind)


def setup_inputs(seed: int = 0) -> dict:
    streams_of = jax.random.split(jax.random.key(seed), 9)
    return {
        "query": draw_query(jax.random.fold_in(streams_of[8], 71), 0),
        "key_new": normal_values(streams_of[1], (BRANCHES, OWN_LEN, KVH * HD), 1.0, 6.0, ((0, 4), (1, 8))),
        "value_new": normal_values(streams_of[2], (BRANCHES, OWN_LEN, KVH * HD), 3.0, 18.0, ((0, 4), (1, 8))),
        "hist_key": draw_hist_key(jax.random.fold_in(streams_of[8], 71), 0),
        "hist_value": normal_values(streams_of[4], (HIST, KVH * HD), 3.0, 18.0, ((0, 8),)),
        "sib_source": draw_sib_source(jax.random.fold_in(streams_of[8], 71), 0),
        "sib_block": draw_sib_block(jax.random.fold_in(streams_of[8], 71), 0),
        "sib_mask": place_ends((jax.random.randint(streams_of[7], (BRANCHES, NBLK, NSIB), 0, 2) < 1).astype(jnp.int32), jax.random.fold_in(streams_of[7], 1), 0, 1),
    }


def visibility(first_row, tile_rows, mask_rows):
    positions = first_row + jnp.arange(tile_rows, dtype=jnp.int32)
    past = jnp.ones((tile_rows, HIST), dtype=jnp.bool_)
    causal = jnp.arange(OWN_LEN, dtype=jnp.int32)[None, :] <= positions[:, None]
    listed = jnp.repeat(mask_rows[positions // BLOCK] == 1, BLOCK, axis=1)
    return jnp.concatenate([past, causal, listed], axis=1)

def reference(query, key_new, value_new, hist_key, hist_value, sib_source, sib_block, sib_mask):
    group_size = QH // KVH
    tile_rows = min(512, OWN_LEN)
    tile_count = OWN_LEN // tile_rows
    score_scale = 1.0 / math.sqrt(HD)
    key_blocks = key_new.reshape(BRANCHES, NBLK, BLOCK, KVH, HD)
    value_blocks = value_new.reshape(BRANCHES, NBLK, BLOCK, KVH, HD)
    results = []
    for branch in range(BRANCHES):
        listed_k = key_blocks[sib_source[branch], sib_block[branch]].reshape(NSIB * BLOCK, KVH, HD)
        listed_v = value_blocks[sib_source[branch], sib_block[branch]].reshape(NSIB * BLOCK, KVH, HD)
        all_keys = jnp.concatenate([hist_key.reshape(HIST, KVH, HD), key_new[branch].reshape(OWN_LEN, KVH, HD), listed_k], 0).transpose(1, 0, 2)
        all_values = jnp.concatenate([hist_value.reshape(HIST, KVH, HD), value_new[branch].reshape(OWN_LEN, KVH, HD), listed_v], 0).transpose(1, 0, 2)
        queries = query[branch].reshape(OWN_LEN, KVH, group_size, HD).transpose(1, 0, 2, 3)
        mask_rows = sib_mask[branch]

        def per_head(operands):
            head_q, head_k, head_v = operands
            key_float = head_k.astype(jnp.float32)
            value_float = head_v.astype(jnp.float32)

            def per_tile(tile_index):
                first_row = tile_index * tile_rows
                tile_q = lax.dynamic_slice_in_dim(head_q, first_row, tile_rows, 0).astype(jnp.float32)
                scores = jnp.einsum('tgd,kd->gtk', tile_q, key_float) * score_scale
                visible = visibility(first_row, tile_rows, mask_rows)
                scores = jnp.where(visible[None], scores, -jnp.inf)
                largest = lax.optimization_barrier(jnp.max(scores, axis=-1, keepdims=True))
                weights = jnp.exp(scores - largest)
                weight_total = lax.optimization_barrier(jnp.sum(weights, axis=-1))
                weight_bf = lax.optimization_barrier(weights.astype(jnp.bfloat16))
                weighted = jnp.einsum('gtk,kd->tgd', weight_bf.astype(jnp.float32), value_float)
                return (weighted / weight_total.T[:, :, None]).astype(jnp.bfloat16)
            tiles = lax.map(per_tile, jnp.arange(tile_count, dtype=jnp.int32))
            return tiles.reshape(OWN_LEN, group_size, HD)
        heads_out = lax.map(per_head, (queries, all_keys, all_values))
        results.append(heads_out.transpose(1, 0, 2, 3).reshape(OWN_LEN, QH * HD))
    return jnp.stack(results)
```

```python
import functools
import math

import jax
import jax.numpy as jnp
from jax import lax
from jax.experimental import pallas as pl
from jax.experimental.pallas import tpu as pltpu
from jax.sharding import PartitionSpec as P

QH = 64
KVH = 8
HD = 128
BLOCK = 256
NSIB = 4
SRCMAX = 2
CORES = 2
GROUP = QH // KVH
HEADS = KVH // CORES
HIDDEN = -1e30
MESH = pl.DeviceIdType.MESH


def kernel(chips, branches, query, key_new, value_new, hist_key, hist_value, source, block, mask,
           out, qbuf, obuf, kv, pick, got, line_held, sib_held, keys, values, scores, bias,
           pair_local, pair_send, pair_recv, q_local, q_send, q_recv,
           line_send, line_recv, sib_send, sib_recv, o_local, o_send, o_recv):
    branch = lax.axis_index("branch")
    place = lax.axis_index("seq")
    chip = place // CORES
    core = place % CORES
    partner = (branch, chip * CORES + 1 - core)
    tokens = query.shape[1]
    hist_rows = hist_key.shape[0]
    hist_all = chips * CORES * hist_rows
    total = keys.shape[0]
    own_at = hist_all
    sib_at = hist_all + chips * BLOCK

    def line_device(step):
        return (branch, ((chip + step) % chips) * CORES + core)

    def sib_device(step):
        return ((branch + step) % branches, place)

    everyone = [partner]
    everyone += [line_device(step) for step in range(1, chips)]
    everyone += [sib_device(step) for step in range(1, branches)]
    barrier = pltpu.get_barrier_semaphore()
    for device in everyone:
        pl.semaphore_signal(barrier, inc=1, device_id=device, device_id_type=MESH)
    pl.semaphore_wait(barrier, len(everyone))

    my_rows = pl.ds(pl.multiple_of(core * tokens, tokens), tokens)
    other_rows = pl.ds(pl.multiple_of((1 - core) * tokens, tokens), tokens)
    my_hist = pl.ds(pl.multiple_of(BLOCK + core * hist_rows, hist_rows), hist_rows)

    def pair_parts(h, owner):
        cols = pl.ds(pl.multiple_of((owner * HEADS + h) * HD, HD), HD)
        return [
            (key_new.at[0, :, cols], kv.at[h, chip, 0, my_rows, :]),
            (value_new.at[0, :, cols], kv.at[h, chip, 1, my_rows, :]),
            (hist_key.at[:, cols], kv.at[h, chip, 0, my_hist, :]),
            (hist_value.at[:, cols], kv.at[h, chip, 1, my_hist, :]),
        ]

    def pair_copies(h):
        here = [
            pltpu.make_async_copy(src, dst, pair_local.at[h, n])
            for n, (src, dst) in enumerate(pair_parts(h, core))
        ]
        there = [
            pltpu.make_async_remote_copy(
                src_ref=src, dst_ref=dst, send_sem=pair_send.at[h, n], recv_sem=pair_recv.at[h, n],
                device_id=partner, device_id_type=MESH)
            for n, (src, dst) in enumerate(pair_parts(h, 1 - core))
        ]
        return here, there

    def q_copies(h):
        def cols(owner):
            return pl.ds(pl.multiple_of((owner * HEADS + h) * GROUP * HD, HD), GROUP * HD)

        here = pltpu.make_async_copy(
            query.at[0, :, cols(core)], qbuf.at[h, my_rows, :], q_local.at[h])
        there = pltpu.make_async_remote_copy(
            src_ref=query.at[0, :, cols(1 - core)], dst_ref=qbuf.at[h, my_rows, :],
            send_sem=q_send.at[h], recv_sem=q_recv.at[h], device_id=partner, device_id_type=MESH)
        return here, there

    def line_copy(h, step):
        return pltpu.make_async_remote_copy(
            src_ref=kv.at[h, chip], dst_ref=kv.at[h, chip],
            send_sem=line_send.at[h, step - 1], recv_sem=line_recv.at[h, step - 1],
            device_id=line_device(step), device_id_type=MESH)

    def sib_copy(h, step):
        return pltpu.make_async_remote_copy(
            src_ref=pick.at[h, step - 1], dst_ref=got.at[h, step - 1],
            send_sem=sib_send.at[h, step - 1], recv_sem=sib_recv.at[h, step - 1],
            device_id=sib_device(step), device_id_type=MESH)

    def o_copies(h):
        cols = pl.ds(pl.multiple_of((core * HEADS + h) * GROUP * HD, HD), GROUP * HD)
        here = pltpu.make_async_copy(obuf.at[h, my_rows, :], out.at[0, :, cols], o_local.at[h])
        there = pltpu.make_async_remote_copy(
            src_ref=obuf.at[h, other_rows, :], dst_ref=out.at[0, :, cols],
            send_sem=o_send.at[h], recv_sem=o_recv.at[h], device_id=partner, device_id_type=MESH)
        return here, there

    @pl.loop(0, HEADS)
    def _(h):
        here, there = pair_copies(h)
        for copy in there + here:
            copy.start()

    @pl.loop(0, HEADS)
    def _(h):
        here, there = pair_copies(h)
        for copy in here:
            copy.wait()
        for copy in there:
            copy.wait_recv()
        for step in range(1, chips):
            line_copy(h, step).start()

    @pl.loop(0, HEADS)
    def _(h):
        here, there = q_copies(h)
        there.start()
        here.start()

    bias[:, 0:hist_all] = jnp.zeros((BLOCK, hist_all), jnp.float32)
    row = lax.broadcasted_iota(jnp.int32, (BLOCK, BLOCK), 0)
    col = lax.broadcasted_iota(jnp.int32, (BLOCK, BLOCK), 1)
    for j in range(chips):
        seen = col + j * BLOCK <= row + chip * BLOCK
        bias[:, own_at + j * BLOCK : own_at + (j + 1) * BLOCK] = jnp.where(seen, 0.0, HIDDEN)
    for i in range(NSIB):
        seen = jnp.broadcast_to(mask[branch, chip, i], (BLOCK, BLOCK)) == 1
        bias[:, sib_at + i * BLOCK : sib_at + (i + 1) * BLOCK] = jnp.where(seen, 0.0, HIDDEN)

    def send_listed(h):
        for step in range(1, chips):
            line_copy(h, step).wait_recv()
        for j in range(chips):
            line_held[j] = kv[h, j, :, 0:BLOCK, :]
        for step in range(1, branches):
            reader = (branch + step) % branches
            count = jnp.int32(0)
            wanted = [jnp.int32(0)] * SRCMAX
            for i in range(NSIB):
                hit = source[reader, i] == branch
                for k in range(SRCMAX):
                    wanted[k] = jnp.where(hit & (count == k), block[reader, i], wanted[k])
                count = count + jnp.where(hit, 1, 0)
            for k in range(SRCMAX):
                pick[h, step - 1, k] = line_held[wanted[k]]
            sib_copy(h, step).start()

    def lay_out(h):
        rows = CORES * hist_rows
        for j in range(chips):
            for kind, whole in enumerate((keys, values)):
                whole[j * rows : (j + 1) * rows, :] = kv[h, j, kind, BLOCK : BLOCK + rows, :]
                whole[own_at + j * BLOCK : own_at + (j + 1) * BLOCK, :] = kv[h, j, kind, 0:BLOCK, :]
        for step in range(1, branches):
            for k in range(SRCMAX):
                sib_held[step - 1, k] = got[h, step - 1, k]
        for i in range(NSIB):
            mine = source[branch, i]
            step = (branch - mine + branches) % branches
            rank = jnp.int32(0)
            for earlier in range(i):
                rank = rank + jnp.where(source[branch, earlier] == mine, 1, 0)
            at = jnp.clip(step - 1, 0, branches - 2)
            rank = jnp.minimum(rank, SRCMAX - 1)
            for kind, whole in enumerate((keys, values)):
                whole[sib_at + i * BLOCK : sib_at + (i + 1) * BLOCK, :] = sib_held[at, rank, kind]

    pieces = [(0, hist_all)] + [(at, BLOCK) for at in range(own_at, total, BLOCK)]
    rate = 1.0 / math.sqrt(HD)

    def attend(h):
        @pl.loop(0, GROUP)
        def _(g):
            cols = pl.ds(pl.multiple_of(g * HD, HD), HD)
            q = qbuf[h, :, cols]
            largest = None
            for at, width in pieces:
                s = lax.dot_general(
                    q, keys[at : at + width, :], (((1,), (1,)), ((), ())),
                    preferred_element_type=jnp.float32)
                s = s + bias[:, at : at + width]
                scores[:, at : at + width] = s
                for lane in range(0, width, HD):
                    part = s[:, lane : lane + HD]
                    largest = part if largest is None else jnp.maximum(largest, part)
            top = jnp.max(largest, axis=1, keepdims=True)
            summed = jnp.zeros((BLOCK, HD), jnp.float32)
            acc = jnp.zeros((BLOCK, HD), jnp.float32)
            for at, width in pieces:
                w = jnp.exp((scores[:, at : at + width] - top) * rate)
                for lane in range(0, width, HD):
                    summed = summed + w[:, lane : lane + HD]
                acc = acc + jnp.dot(
                    w.astype(jnp.bfloat16), values[at : at + width, :],
                    preferred_element_type=jnp.float32)
            weight_total = jnp.sum(summed, axis=1, keepdims=True)
            obuf[h, :, cols] = (acc / weight_total).astype(jnp.bfloat16)

    send_listed(0)

    @pl.loop(0, HEADS)
    def _(h):
        @pl.when(h + 1 < HEADS)
        def _():
            send_listed(h + 1)

        here, there = q_copies(h)
        here.wait()
        there.wait_recv()
        for step in range(1, branches):
            sib_copy(h, step).wait_recv()
        lay_out(h)
        attend(h)
        here, there = o_copies(h)
        there.start()
        here.start()

    @pl.loop(0, HEADS)
    def _(h):
        for copy in pair_copies(h)[1]:
            copy.wait_send()
        q_copies(h)[1].wait_send()
        for step in range(1, chips):
            line_copy(h, step).wait_send()
        for step in range(1, branches):
            sib_copy(h, step).wait_send()
        here, there = o_copies(h)
        here.wait()
        there.wait()


def body(query, key_new, value_new, hist_key, hist_value, sib_source, sib_block, sib_mask):
    chips = lax.axis_size("seq") // CORES
    branches = lax.axis_size("branch")
    hist_rows = hist_key.shape[0]
    hist_all = hist_rows * chips * CORES
    total = hist_all + chips * BLOCK + NSIB * BLOCK
    dma = pltpu.SemaphoreType.DMA
    anywhere = pl.BlockSpec(memory_space=pl.ANY)
    scalars = pl.BlockSpec(memory_space=pltpu.SMEM)
    return pl.pallas_call(
        functools.partial(kernel, chips, branches),
        out_shape=jax.ShapeDtypeStruct(query.shape, jnp.bfloat16),
        in_specs=[anywhere] * 5 + [scalars] * 3,
        out_specs=anywhere,
        scratch_shapes=[
            pltpu.VMEM((HEADS, BLOCK, GROUP * HD), jnp.bfloat16),
            pltpu.VMEM((HEADS, BLOCK, GROUP * HD), jnp.bfloat16),
            pltpu.VMEM((HEADS, chips, 2, BLOCK + CORES * hist_rows, HD), jnp.bfloat16),
            pltpu.VMEM((HEADS, branches - 1, SRCMAX, 2, BLOCK, HD), jnp.bfloat16),
            pltpu.VMEM((HEADS, branches - 1, SRCMAX, 2, BLOCK, HD), jnp.bfloat16),
            pltpu.VMEM((chips, 2, BLOCK, HD), jnp.bfloat16),
            pltpu.VMEM((branches - 1, SRCMAX, 2, BLOCK, HD), jnp.bfloat16),
            pltpu.VMEM((total, HD), jnp.bfloat16),
            pltpu.VMEM((total, HD), jnp.bfloat16),
            pltpu.VMEM((BLOCK, total), jnp.float32),
            pltpu.VMEM((BLOCK, total), jnp.float32),
            dma((HEADS, 4)), dma((HEADS, 4)), dma((HEADS, 4)),
            dma((HEADS,)), dma((HEADS,)), dma((HEADS,)),
            dma((HEADS, chips - 1)), dma((HEADS, chips - 1)),
            dma((HEADS, branches - 1)), dma((HEADS, branches - 1)),
            dma((HEADS,)), dma((HEADS,)), dma((HEADS,)),
        ],
        compiler_params=pltpu.CompilerParams(
            collective_id=0, has_side_effects=True, vmem_limit_bytes=56 * 1024 * 1024),
        cost_estimate=pl.CostEstimate(
            flops=4 * HEADS * GROUP * BLOCK * total * HD,
            bytes_accessed=2 * query.size * 2, transcendentals=HEADS * GROUP * BLOCK * total),
    )(query, key_new, value_new, hist_key, hist_value, sib_source, sib_block, sib_mask)


def solution(mesh):
    in_specs = (
        P("branch", "seq", None),
        P("branch", "seq", None),
        P("branch", "seq", None),
        P("seq", None),
        P("seq", None),
        P(),
        P(),
        P(),
    )
    out_specs = P("branch", "seq", None)
    return jax.shard_map(body, mesh=mesh, in_specs=in_specs, out_specs=out_specs, check_vma=False)
```

```python
import functools
import math

import jax
import jax.numpy as jnp
from jax import lax
from jax.experimental import pallas as pl
from jax.experimental.pallas import tpu as pltpu
from jax.sharding import PartitionSpec as P

QH = 64
KVH = 8
HD = 128
BLOCK = 256
NSIB = 4
SRCMAX = 2
CORES = 2
GROUP = QH // KVH
HEADS = KVH // CORES
HIDDEN = -1e30
MESH = pl.DeviceIdType.MESH


def kernel(chips, branches, query, key_new, value_new, hist_key, hist_value, source, block, mask,
           out, qbuf, obuf, kv, pick, got, line_held, sib_held, keys, values, scores, bias,
           tops, sums, accs,
           pair_local, pair_send, pair_recv, q_local, q_send, q_recv,
           line_send, line_recv, sib_send, sib_recv, o_local, o_send, o_recv):
    branch = lax.axis_index("branch")
    place = lax.axis_index("seq")
    chip = place // CORES
    core = place % CORES
    partner = (branch, chip * CORES + 1 - core)
    tokens = query.shape[1]
    hist_rows = hist_key.shape[0]
    hist_all = chips * CORES * hist_rows
    total = keys.shape[0]
    own_at = hist_all
    sib_at = hist_all + chips * BLOCK

    def line_device(step):
        return (branch, ((chip + step) % chips) * CORES + core)

    def sib_device(step):
        return ((branch + step) % branches, place)

    everyone = [partner]
    everyone += [line_device(step) for step in range(1, chips)]
    everyone += [sib_device(step) for step in range(1, branches)]
    barrier = pltpu.get_barrier_semaphore()
    for device in everyone:
        pl.semaphore_signal(barrier, inc=1, device_id=device, device_id_type=MESH)
    pl.semaphore_wait(barrier, len(everyone))

    my_rows = pl.ds(pl.multiple_of(core * tokens, tokens), tokens)
    other_rows = pl.ds(pl.multiple_of((1 - core) * tokens, tokens), tokens)
    my_hist = pl.ds(pl.multiple_of(BLOCK + core * hist_rows, hist_rows), hist_rows)

    def pair_parts(h, owner):
        cols = pl.ds(pl.multiple_of((owner * HEADS + h) * HD, HD), HD)
        return [
            (key_new.at[0, :, cols], kv.at[h, chip, 0, my_rows, :]),
            (value_new.at[0, :, cols], kv.at[h, chip, 1, my_rows, :]),
            (hist_key.at[:, cols], kv.at[h, chip, 0, my_hist, :]),
            (hist_value.at[:, cols], kv.at[h, chip, 1, my_hist, :]),
        ]

    def pair_copies(h):
        here = [
            pltpu.make_async_copy(src, dst, pair_local.at[h, n])
            for n, (src, dst) in enumerate(pair_parts(h, core))
        ]
        there = [
            pltpu.make_async_remote_copy(
                src_ref=src, dst_ref=dst, send_sem=pair_send.at[h, n], recv_sem=pair_recv.at[h, n],
                device_id=partner, device_id_type=MESH)
            for n, (src, dst) in enumerate(pair_parts(h, 1 - core))
        ]
        return here, there

    def q_copies(h):
        def cols(owner):
            return pl.ds(pl.multiple_of((owner * HEADS + h) * GROUP * HD, HD), GROUP * HD)

        here = pltpu.make_async_copy(
            query.at[0, :, cols(core)], qbuf.at[h, my_rows, :], q_local.at[h])
        there = pltpu.make_async_remote_copy(
            src_ref=query.at[0, :, cols(1 - core)], dst_ref=qbuf.at[h, my_rows, :],
            send_sem=q_send.at[h], recv_sem=q_recv.at[h], device_id=partner, device_id_type=MESH)
        return here, there

    def line_copy(h, step):
        return pltpu.make_async_remote_copy(
            src_ref=kv.at[h, chip], dst_ref=kv.at[h, chip],
            send_sem=line_send.at[h, step - 1], recv_sem=line_recv.at[h, step - 1],
            device_id=line_device(step), device_id_type=MESH)

    def sib_copy(h, step):
        return pltpu.make_async_remote_copy(
            src_ref=pick.at[h, step - 1], dst_ref=got.at[h, step - 1],
            send_sem=sib_send.at[h, step - 1], recv_sem=sib_recv.at[h, step - 1],
            device_id=sib_device(step), device_id_type=MESH)

    def o_copies(h):
        cols = pl.ds(pl.multiple_of((core * HEADS + h) * GROUP * HD, HD), GROUP * HD)
        here = pltpu.make_async_copy(obuf.at[h, my_rows, :], out.at[0, :, cols], o_local.at[h])
        there = pltpu.make_async_remote_copy(
            src_ref=obuf.at[h, other_rows, :], dst_ref=out.at[0, :, cols],
            send_sem=o_send.at[h], recv_sem=o_recv.at[h], device_id=partner, device_id_type=MESH)
        return here, there

    @pl.loop(0, HEADS)
    def _(h):
        here, there = pair_copies(h)
        for copy in there + here:
            copy.start()

    @pl.loop(0, HEADS)
    def _(h):
        here, there = pair_copies(h)
        for copy in here:
            copy.wait()
        for copy in there:
            copy.wait_recv()

        @pl.when(h == 0)
        def _():
            for step in range(1, chips):
                line_copy(h, step).start()

    @pl.loop(0, HEADS)
    def _(h):
        here, there = q_copies(h)
        there.start()
        here.start()

    row = lax.broadcasted_iota(jnp.int32, (BLOCK, BLOCK), 0)
    col = lax.broadcasted_iota(jnp.int32, (BLOCK, BLOCK), 1)
    for j in range(chips):
        seen = col + j * BLOCK <= row + chip * BLOCK
        bias[:, j * BLOCK : (j + 1) * BLOCK] = jnp.where(seen, 0.0, HIDDEN)

    def send_line(h):
        for step in range(1, chips):
            line_copy(h, step).start()

    def line_left(h):
        for step in range(1, chips):
            line_copy(h, step).wait_send()

    def send_listed(h):
        for step in range(1, chips):
            line_copy(h, step).wait_recv()
        for j in range(chips):
            line_held[j] = kv[h, j, :, 0:BLOCK, :]
        for step in range(1, branches):
            reader = (branch + step) % branches
            count = jnp.int32(0)
            wanted = [jnp.int32(0)] * SRCMAX
            for i in range(NSIB):
                hit = source[reader, i] == branch
                for k in range(SRCMAX):
                    wanted[k] = jnp.where(hit & (count == k), block[reader, i], wanted[k])
                count = count + jnp.where(hit, 1, 0)
            for k in range(SRCMAX):
                pick[h, step - 1, k] = line_held[wanted[k]]
            sib_copy(h, step).start()

    def lay_out_own(h):
        rows = CORES * hist_rows
        for j in range(chips):
            for kind, whole in enumerate((keys, values)):
                whole[j * rows : (j + 1) * rows, :] = kv[h, j, kind, BLOCK : BLOCK + rows, :]
                whole[own_at + j * BLOCK : own_at + (j + 1) * BLOCK, :] = kv[h, j, kind, 0:BLOCK, :]

    def lay_out_listed(h):
        for step in range(1, branches):
            for k in range(SRCMAX):
                sib_held[step - 1, k] = got[h, step - 1, k]
        for i in range(NSIB):
            mine = source[branch, i]
            step = (branch - mine + branches) % branches
            rank = jnp.int32(0)
            for earlier in range(i):
                rank = rank + jnp.where(source[branch, earlier] == mine, 1, 0)
            at = jnp.clip(step - 1, 0, branches - 2)
            rank = jnp.minimum(rank, SRCMAX - 1)
            for kind, whole in enumerate((keys, values)):
                whole[sib_at + i * BLOCK : sib_at + (i + 1) * BLOCK, :] = sib_held[at, rank, kind]

    own_pieces = [(0, hist_all)] + [(at, BLOCK) for at in range(own_at, sib_at, BLOCK)]
    sib_pieces = [(at, BLOCK) for at in range(sib_at, total, BLOCK)]
    rate = math.log2(math.e) / math.sqrt(HD)
    shown = [jnp.where(mask[branch, chip, i] == 1, 0.0, HIDDEN) for i in range(NSIB)]

    def score(q, pieces, largest):
        for at, width in pieces:
            s = lax.dot_general(
                q, keys[at : at + width, :], (((1,), (1,)), ((), ())),
                preferred_element_type=jnp.float32)
            if at >= sib_at:
                s = s + shown[(at - sib_at) // BLOCK]
            elif at >= own_at:
                s = s + bias[:, at - own_at : at - own_at + width]
            scores[:, at : at + width] = s
            for lane in range(0, width, HD):
                part = s[:, lane : lane + HD]
                largest = part if largest is None else jnp.maximum(largest, part)
        return largest

    def weigh(pieces, top, summed, acc):
        for at, width in pieces:
            w = jnp.exp2((scores[:, at : at + width] - top) * rate)
            for lane in range(0, width, HD):
                summed = summed + w[:, lane : lane + HD]
            acc = acc + jnp.dot(
                w.astype(jnp.bfloat16), values[at : at + width, :],
                preferred_element_type=jnp.float32)
        return summed, acc

    def attend_own(h):
        @pl.loop(0, GROUP)
        def _(g):
            q = qbuf[h, :, pl.ds(pl.multiple_of(g * HD, HD), HD)]
            largest = score(q, own_pieces, None)
            top = jnp.max(largest, axis=1, keepdims=True)
            zero = jnp.zeros((BLOCK, HD), jnp.float32)
            summed, acc = weigh(own_pieces, top, zero, zero)
            tops[g] = jnp.broadcast_to(top, (BLOCK, HD))
            sums[g] = summed
            accs[g] = acc

    def attend_listed(h):
        @pl.loop(0, GROUP)
        def _(g):
            cols = pl.ds(pl.multiple_of(g * HD, HD), HD)
            before = tops[g]
            largest = score(qbuf[h, :, cols], sib_pieces, before)
            top = jnp.max(largest, axis=1, keepdims=True)
            shrink = jnp.exp2((before - top) * rate)
            summed, acc = weigh(sib_pieces, top, sums[g] * shrink, accs[g] * shrink)
            weight_total = jnp.sum(summed, axis=1, keepdims=True)
            obuf[h, :, cols] = (acc / weight_total).astype(jnp.bfloat16)

    line_left(0)
    send_line(1)
    send_listed(0)

    @pl.loop(0, HEADS)
    def _(h):
        here, there = q_copies(h)
        here.wait()
        there.wait_recv()
        lay_out_own(h)
        attend_own(h)

        @pl.when(h + 1 < HEADS)
        def _():
            line_left(h + 1)

            @pl.when(h + 2 < HEADS)
            def _():
                send_line(h + 2)

            send_listed(h + 1)

        for step in range(1, branches):
            sib_copy(h, step).wait_recv()
        lay_out_listed(h)
        attend_listed(h)
        here, there = o_copies(h)
        there.start()
        here.start()

    @pl.loop(0, HEADS)
    def _(h):
        for copy in pair_copies(h)[1]:
            copy.wait_send()
        q_copies(h)[1].wait_send()
        for step in range(1, branches):
            sib_copy(h, step).wait_send()
        here, there = o_copies(h)
        here.wait()
        there.wait()


def body(query, key_new, value_new, hist_key, hist_value, sib_source, sib_block, sib_mask):
    chips = lax.axis_size("seq") // CORES
    branches = lax.axis_size("branch")
    hist_rows = hist_key.shape[0]
    hist_all = hist_rows * chips * CORES
    total = hist_all + chips * BLOCK + NSIB * BLOCK
    dma = pltpu.SemaphoreType.DMA
    anywhere = pl.BlockSpec(memory_space=pl.ANY)
    scalars = pl.BlockSpec(memory_space=pltpu.SMEM)
    return pl.pallas_call(
        functools.partial(kernel, chips, branches),
        out_shape=jax.ShapeDtypeStruct(query.shape, jnp.bfloat16),
        in_specs=[anywhere] * 5 + [scalars] * 3,
        out_specs=anywhere,
        scratch_shapes=[
            pltpu.VMEM((HEADS, BLOCK, GROUP * HD), jnp.bfloat16),
            pltpu.VMEM((HEADS, BLOCK, GROUP * HD), jnp.bfloat16),
            pltpu.VMEM((HEADS, chips, 2, BLOCK + CORES * hist_rows, HD), jnp.bfloat16),
            pltpu.VMEM((HEADS, branches - 1, SRCMAX, 2, BLOCK, HD), jnp.bfloat16),
            pltpu.VMEM((HEADS, branches - 1, SRCMAX, 2, BLOCK, HD), jnp.bfloat16),
            pltpu.VMEM((chips, 2, BLOCK, HD), jnp.bfloat16),
            pltpu.VMEM((branches - 1, SRCMAX, 2, BLOCK, HD), jnp.bfloat16),
            pltpu.VMEM((total, HD), jnp.bfloat16),
            pltpu.VMEM((total, HD), jnp.bfloat16),
            pltpu.VMEM((BLOCK, total), jnp.float32),
            pltpu.VMEM((BLOCK, chips * BLOCK), jnp.float32),
            pltpu.VMEM((GROUP, BLOCK, HD), jnp.float32),
            pltpu.VMEM((GROUP, BLOCK, HD), jnp.float32),
            pltpu.VMEM((GROUP, BLOCK, HD), jnp.float32),
            dma((HEADS, 4)), dma((HEADS, 4)), dma((HEADS, 4)),
            dma((HEADS,)), dma((HEADS,)), dma((HEADS,)),
            dma((HEADS, chips - 1)), dma((HEADS, chips - 1)),
            dma((HEADS, branches - 1)), dma((HEADS, branches - 1)),
            dma((HEADS,)), dma((HEADS,)), dma((HEADS,)),
        ],
        compiler_params=pltpu.CompilerParams(
            collective_id=0, has_side_effects=True, vmem_limit_bytes=56 * 1024 * 1024),
        cost_estimate=pl.CostEstimate(
            flops=4 * HEADS * GROUP * BLOCK * total * HD,
            bytes_accessed=2 * query.size * 2, transcendentals=HEADS * GROUP * BLOCK * total),
    )(query, key_new, value_new, hist_key, hist_value, sib_source, sib_block, sib_mask)


def solution(mesh):
    in_specs = (
        P("branch", "seq", None),
        P("branch", "seq", None),
        P("branch", "seq", None),
        P("seq", None),
        P("seq", None),
        P(),
        P(),
        P(),
    )
    out_specs = P("branch", "seq", None)
    return jax.shard_map(body, mesh=mesh, in_specs=in_specs, out_specs=out_specs, check_vma=False)
```
